512 devices in a mesh: dp: 16 (over y_hi, x), tensor: 32 (over z, y_lo, core).
Axes of the slice: x: 4, y: 8 (y_hi: 4, y_lo: 2; y = y_hi * 2 + y_lo), z: 8, core: 2. Of those that a mesh axis runs over, the one named last changes fastest.
Arguments:
- grad_a_parts: float32 [16, 512, 4096], P('dp', None, 'tensor'), may hold values from -0.125 to 0.125
- grad_b_parts: float32 [16, 12288, 32], P('dp', 'tensor'), may hold values from -0.125 to 0.125
- factor_a: float32 [512, 4096], P('dp', 'tensor'), may hold values from -0.25 to 0.25
- moment_a: float32 [512, 4096], P('dp', 'tensor'), may hold values from -0.25 to 0.25
- factor_b: float32 [12288, 32], P(('tensor', 'dp')), may hold values from -0.25 to 0.25
- moment_b: float32 [12288, 32], P(('tensor', 'dp')), may hold values from -0.25 to 0.25
- base_down: bfloat16 [12288, 4096], P('tensor'), may hold values from -0.21875 to 0.21875
- slot_hidden: bfloat16 [3072, 12288], P('dp', 'tensor'), may hold values from -6 to 6
- expert_ids: int32 [4096, 8], P('dp'), may hold values from 0 to 15, all different within a row; in each aligned block of 256 rows (0 to 255, 256 to 511, ...) at most 192 rows name the same one
- combine_weights: float32 [4096, 8], P('dp'), may hold values from 0.05 to 0.5
Outputs:
- stepped_factor_a: float32 [512, 4096], P('dp', 'tensor')
- stepped_factor_b: float32 [12288, 32], P(('tensor', 'dp'))
- scored: bfloat16 [4096, 4096], P(('dp', 'tensor'))
The draws below stay inside these ranges and needn't reach their ends.
Inputs may be any that keep to these rules, and one draw needn't show every extreme that they name: `expert_ids`: within each replica group's 256 tokens no expert is chosen more than 192 times, a bound that some block reaches; slots of an expert past its count in a group are never read.
All inputs are finite; a program needn't handle non-finite values.
Results may differ from the reference program's by a relative error of at most 0.0054.
Values may be sent and summed in bfloat16 or wider, within the bound.
No kernel may reach another device: no remote copies, remote signals or barrier semaphores. Data moves between devices by JAX's collectives and lax.ppermute only.
A program may use at most 64 MiB of HBM per device.

```python
import math
import jax
import jax.numpy as jnp
import numpy as np
from jax import lax

D = 4096
HALF_HIDDEN = 768
ADAPTER_RANK = 32
EXPERTS = 16
TOPK = 8
TOK_GROUP = 256
CAP = 192
TOKENS = 4096
N_DP = 16


def strengthened(result, own_key, source, target, parts, factor):
    owner, partner = [(jnp.arange(result.shape[dim]) // (result.shape[dim] // parts)).reshape([-1 if axis == dim else 1 for axis in range(result.ndim)]) for dim in (source, target)]
    chosen = jax.random.permutation(own_key, parts)[partner]
    strong = (owner == chosen) | (owner == (partner + parts // 2) % parts)
    return jnp.where(strong, factor * result, result)


def level_of(stream_key, extent, cuts, smallest, largest):
    level, own = 1.0, jax.random.fold_in(stream_key, 6)
    for position, blocks in cuts:
        draws = jnp.exp(jax.random.uniform(jax.random.fold_in(own, position), (blocks,), jnp.float32, smallest / len(cuts), largest / len(cuts)))
        level = level * jnp.repeat(draws, extent[position] // blocks).reshape([-1 if axis == position else 1 for axis in range(len(extent))])
    return level


def shared_out(own_key, own, number, rows, amount, top, most, lean):
    sequence = jax.random.permutation(own_key, amount)
    packed, common = portions_of(amount, rows * top, most, lean, True), portions_of(amount, rows * top, most, lean, False)
    places = jnp.arange(amount)

    def named(sizes, offset_by):
        used = int((sizes > 0).sum())
        fixed = max(1, used // 4)
        shifted = fixed + (places - fixed + offset_by * (used - fixed)) % max(1, amount - fixed)
        return jnp.zeros((amount,), jnp.int32).at[sequence[jnp.where(places < fixed, places, shifted)]].set(jnp.asarray(sizes, jnp.int32))

    sizes = jnp.where(number % 4 == 0, named(packed, number // 4), named(common, number - number // 4 - 1))
    mixed = jax.random.permutation(jax.random.fold_in(own, 3), amount)
    giver, taker = mixed[0:amount // 2 * 2:2], mixed[1:amount // 2 * 2:2]
    slack = jnp.minimum(sizes[giver] - 1, most - sizes[taker]) // 2
    slack = jnp.where((giver == sequence[0]) | (taker == sequence[0]) | (sizes[taker] == 0), 0, jnp.maximum(slack, 0))
    shifted = jax.random.randint(jax.random.fold_in(own, 4), (amount // 2,), 0, 1 << 20) % (slack + 1)
    sizes = sizes.at[giver].add(-shifted).at[taker].add(shifted)
    members = jnp.searchsorted(jnp.cumsum(sizes), jnp.arange(rows * top), side="right").astype(jnp.int32)
    grid = members.reshape(top, rows).T
    grid = grid[jax.random.permutation(jax.random.fold_in(own, 1), rows)]
    offset_by = jax.random.randint(jax.random.fold_in(own, 2), (rows, 1), 0, top)
    return jnp.take_along_axis(grid, (jnp.arange(top)[None, :] + offset_by) % top, axis=1)


def portions_of(amount, total, bound, skew, full):
    portions = [(1 << 20) // math.isqrt(rank ** skew) + 1 for rank in range(1, amount + 1)]
    largest = bound if full else min(bound, max(-(-total // amount), total * portions[0] // sum(portions)))
    least = 1 if total - largest >= amount - 1 else 0
    holding, spare = [largest] + [least] * (amount - 1), total - largest - least * (amount - 1)
    while spare > 0:
        candidates = [i for i in range(1, amount) if holding[i] < largest] or [i for i in range(1, amount) if holding[i] < bound]
        whole, left = sum([portions[i] for i in candidates]), spare
        for i in candidates:
            addition = min(bound - holding[i], max(1, left * portions[i] // whole), spare)
            holding[i] = holding[i] + addition
            spare = spare - addition
    return np.array(holding)


def gaussian(rng, extent, width, reach, pieces=(), held_as=jnp.bfloat16):
    array = jax.random.normal(rng, extent, jnp.float32) * width
    if len(pieces) > 0:
        array = level_of(rng, extent, pieces, -0.22, 0.18) * array
    return jnp.clip(array, min=-reach, max=reach).astype(held_as)


def heavy_noise(stream_key, shape, deviation, bound, split, heavy, kind=jnp.bfloat16):
    array = deviation * jax.random.normal(stream_key, shape, jnp.float32)
    if split:
        array = array * level_of(stream_key, shape, split, -0.22, 0.18)
    return jnp.clip(strengthened(array, jax.random.fold_in(stream_key, 3), *heavy), -bound, bound).astype(kind)


def setup_inputs(seed: int = 0) -> dict:
    keys = jax.random.split(jax.random.key(seed), 11)
    grad_a_parts = heavy_noise(keys[0], (N_DP, EXPERTS * ADAPTER_RANK, D), 0.015, 0.125, ((0, 16), (2, 32)), (0, 1, 16, 2.0), jnp.float32)
    grad_b_parts = heavy_noise(keys[1], (N_DP, EXPERTS * HALF_HIDDEN, ADAPTER_RANK), 0.015, 0.125, ((0, 16), (1, 32)), (0, 1, 16, 2.0), jnp.float32)
    factor_a = gaussian(keys[2], (EXPERTS * ADAPTER_RANK, D), 0.04, 0.25, ((0, 16), (1, 32)), jnp.float32)
    moment_a = gaussian(keys[3], (EXPERTS * ADAPTER_RANK, D), 0.04, 0.25, ((0, 16), (1, 32)), jnp.float32)
    factor_b = gaussian(keys[4], (EXPERTS * HALF_HIDDEN, ADAPTER_RANK), 0.04, 0.25, ((0, 512),), jnp.float32)
    moment_b = gaussian(keys[5], (EXPERTS * HALF_HIDDEN, ADAPTER_RANK), 0.04, 0.25, ((0, 512),), jnp.float32)
    base_down = gaussian(keys[6], (EXPERTS * HALF_HIDDEN, D), HALF_HIDDEN ** -0.5, 0.21875, ((0, 32),))
    slot_hidden = gaussian(keys[7], (N_DP * CAP, EXPERTS * HALF_HIDDEN), 1.0, 6.0, ((0, 16), (1, 32)))
    expert_ids_keys = jax.random.split(jax.random.fold_in(keys[8], 1), TOKENS // TOK_GROUP)
    expert_ids_turns = jax.random.permutation(jax.random.fold_in(keys[8], 3), TOKENS // TOK_GROUP)
    expert_ids = jax.vmap(lambda own, number: shared_out(jax.random.fold_in(keys[8], 2), own, number, TOK_GROUP, EXPERTS, TOPK, CAP, 2))(expert_ids_keys, expert_ids_turns).reshape((TOKENS, TOPK))
    combine_weights = jnp.clip(0.05 + 0.45 * jax.random.uniform(keys[9], (TOKENS, TOPK), jnp.float32) ** level_of(keys[9], (TOKENS, TOPK), ((0, 16),), -0.2, 0.2), 0.05, 0.5)
    return {"grad_a_parts": grad_a_parts, "grad_b_parts": grad_b_parts, "factor_a": factor_a, "moment_a": moment_a, "factor_b": factor_b, "moment_b": moment_b, "base_down": base_down, "slot_hidden": slot_hidden, "expert_ids": expert_ids, "combine_weights": combine_weights}


MOMENTUM = 0.9
RATE = 0.5


def slot_positions(expert_ids):
    flat = expert_ids.reshape(-1)
    onehot = (flat[:, None] == jnp.arange(EXPERTS, dtype=jnp.int32)[None, :]).astype(jnp.int32)
    before = jnp.cumsum(onehot, axis=0) - onehot
    return jnp.sum(before * onehot, axis=1).reshape(expert_ids.shape).astype(jnp.int32)


def combine_table(expert_ids, slots, weights, expert_index, slot_count):
    columns = jnp.arange(slot_count, dtype=jnp.int32)
    hit = (expert_ids == expert_index)[:, :, None] & (slots[:, :, None] == columns[None, None, :])
    return jnp.sum(jnp.where(hit, weights[:, :, None], jnp.zeros((), weights.dtype)), axis=1)


def reference(grad_a_parts, grad_b_parts, factor_a, moment_a, factor_b, moment_b, base_down, slot_hidden, expert_ids, combine_weights):
    grad_a = jnp.sum(grad_a_parts, axis=0)
    grad_b = jnp.sum(grad_b_parts, axis=0)
    stepped_factor_a = factor_a - RATE * (MOMENTUM * moment_a + grad_a)
    stepped_factor_b = factor_b - RATE * (MOMENTUM * moment_b + grad_b)
    adapter_factor_a = stepped_factor_a.astype(jnp.bfloat16)
    adapter_factor_b = stepped_factor_b.astype(jnp.bfloat16)

    def merge_one(expert_index):
        base = lax.dynamic_slice_in_dim(base_down, expert_index * HALF_HIDDEN, HALF_HIDDEN, 0)
        left_factor = lax.dynamic_slice_in_dim(adapter_factor_b, expert_index * HALF_HIDDEN, HALF_HIDDEN, 0)
        right_factor = lax.dynamic_slice_in_dim(adapter_factor_a, expert_index * ADAPTER_RANK, ADAPTER_RANK, 0)
        update = jnp.dot(left_factor, right_factor, preferred_element_type=jnp.float32)
        return (base.astype(jnp.float32) + update).astype(jnp.bfloat16)

    merged = lax.map(merge_one, jnp.arange(EXPERTS, dtype=jnp.int32))
    groups = expert_ids.shape[0] // TOK_GROUP
    hidden_groups = slot_hidden.reshape(groups, CAP, EXPERTS * HALF_HIDDEN)
    id_groups = expert_ids.reshape(groups, TOK_GROUP, TOPK)
    weight_groups = combine_weights.reshape(groups, TOK_GROUP, TOPK)

    def group_out(inputs):
        hidden, ids, weights = inputs
        slots = slot_positions(ids)

        def per_expert(total, expert_index):
            block = lax.dynamic_slice_in_dim(hidden, expert_index * HALF_HIDDEN, HALF_HIDDEN, 1)
            outputs = jnp.dot(block, merged[expert_index], preferred_element_type=jnp.float32)
            table = combine_table(ids, slots, weights, expert_index, CAP)
            return total + jnp.dot(table, outputs, precision=lax.Precision.HIGHEST), None

        start = jnp.zeros((TOK_GROUP, D), jnp.float32)
        total, _ = lax.scan(per_expert, start, jnp.arange(EXPERTS, dtype=jnp.int32))
        return total.astype(jnp.bfloat16)

    scored = lax.map(group_out, (hidden_groups, id_groups, weight_groups))
    return stepped_factor_a, stepped_factor_b, scored.reshape(groups * TOK_GROUP, D)
```

```python
import jax
import jax.numpy as jnp
from jax import lax
from jax.experimental import pallas as pl
from jax.experimental.pallas import tpu as pltpu
from jax.sharding import PartitionSpec as P

MOMENTUM = 0.9
RATE = 0.5
RANK = 32
B_ROWS = 24
CHUNK = 48
OWNERS = 16
CHIPS = 16
SLOTS = 192
TOKENS = 256
HALF = 128
WIDTH = 4096
TILE = 1024
F32 = jnp.float32
BF16 = jnp.bfloat16


def pack_b(block):
    tail = jnp.concatenate([block[16:24], jnp.zeros((8, RANK), F32)], axis=0)
    return jnp.concatenate([block[0:16], tail, jnp.zeros((16, 64), F32)], axis=1)


def pack_kernel(grad_a, grad_b, out):
    for owner in range(OWNERS):
        out[owner, 0:RANK, :] = grad_a[0, owner * RANK : (owner + 1) * RANK, :].astype(BF16)
        block = grad_b[0, owner * B_ROWS : (owner + 1) * B_ROWS, :]
        out[owner, RANK:CHUNK, :] = pack_b(block).astype(BF16)


def step_kernel(parts, factor_a, moment_a, factor_b, moment_b, new_a, new_b, send_a, send_b):
    total = parts[0].astype(F32)
    for owner in range(1, OWNERS):
        total = total + parts[owner].astype(F32)
    stepped_a = factor_a[...] - RATE * (MOMENTUM * moment_a[...] + total[0:RANK])
    grad_b = jnp.concatenate([total[RANK:CHUNK, 0:32], total[RANK : RANK + 8, 32:64]], axis=0)
    stepped_b = factor_b[...] - RATE * (MOMENTUM * moment_b[...] + grad_b)
    new_a[...] = stepped_a
    new_b[...] = stepped_b
    send_a[...] = stepped_a.astype(BF16)
    send_b[...] = pack_b(stepped_b).astype(BF16)


def base_kernel(ids, weights, hidden, base, send, own, rows, row_weights, slot_scr, weight_scr, order_scr):
    index = lax.axis_index("tensor")
    expert, core = index // 2, index % 2

    @pl.when(pl.program_id(0) == 0)
    def _():
        named = ids[...] == expert
        hit = jnp.sum(jnp.where(named, 1.0, 0.0), axis=1, keepdims=True)
        weight = jnp.sum(jnp.where(named, weights[...], 0.0), axis=1, keepdims=True)
        hit = jnp.broadcast_to(hit, (TOKENS, 128))
        row = lax.broadcasted_iota(jnp.int32, (TOKENS, TOKENS), 0)
        column = lax.broadcasted_iota(jnp.int32, (TOKENS, TOKENS), 1)
        earlier = jnp.where(column < row, 1.0, 0.0).astype(BF16)
        before = jnp.dot(earlier, hit.astype(BF16), preferred_element_type=F32)
        slot_scr[...] = jnp.where(hit > 0.5, before, -1.0)
        weight_scr[...] = jnp.broadcast_to(weight, (TOKENS, 128))
        for half in range(2):
            side = 1 - core if half == 0 else core
            for chip in range(CHIPS):
                source = pl.ds(pl.multiple_of(chip * 16 + side * 8, 8), 8)
                target = pl.ds(half * HALF + chip * 8, 8)
                order_scr[target, :] = slot_scr[source, :]
                row_weights[target, :] = weight_scr[source, :]
        slots = lax.broadcasted_iota(jnp.int32, (TOKENS, SLOTS), 1)
        chosen = order_scr[:, 0:1].astype(jnp.int32) == slots
        chosen = jnp.where(chosen, 1.0, 0.0).astype(BF16)
        rows[...] = jnp.dot(chosen, hidden[...], preferred_element_type=F32).astype(BF16)

    part = jnp.dot(rows[...], base[...], preferred_element_type=F32) * row_weights[:, 0:1]
    send[...] = part[0:HALF].astype(BF16)
    own[...] = part[HALF:TOKENS].astype(BF16)


def low_rank_kernel(gathered, rows, row_weights, packet, own, b_scr):
    for owner in range(OWNERS):
        packet[owner * RANK : (owner + 1) * RANK, :] = gathered[owner, 0:RANK, :]
        block = gathered[owner, RANK:CHUNK, :].astype(F32)
        b_scr[owner * B_ROWS : owner * B_ROWS + 16, :] = block[:, 0:32]
        b_scr[owner * B_ROWS + 16 : (owner + 1) * B_ROWS, :] = block[0:8, 32:64]
    low = jnp.dot(rows[...], b_scr[...].astype(BF16), preferred_element_type=F32)
    low = low * row_weights[:, 0:1]
    pieces = [low[at : at + 32] for at in range(0, HALF, 32)]
    packet[OWNERS * RANK :, :] = jnp.concatenate(pieces, axis=1).astype(BF16)
    own[...] = low[HALF:TOKENS]


def join_kernel(packets, low, own, other, out):
    core = lax.axis_index("tensor") % 2
    received = packets[1 - core, OWNERS * RANK :, :].astype(F32)
    received = jnp.concatenate([received[:, at : at + 32] for at in range(0, 128, 32)], axis=0)
    low = (low[...] + received).astype(BF16)
    step = pl.program_id(0)
    blocks = TILE // 256
    for block in range(blocks):
        at = pl.ds(pl.multiple_of((step * blocks + block) * RANK, RANK), RANK)
        factor = jnp.concatenate([packets[0, at, :], packets[1, at, :]], axis=1)
        columns = slice(block * 256, (block + 1) * 256)
        update = jnp.dot(low, factor, preferred_element_type=F32)
        total = own[:, columns].astype(F32) + other[:, columns].astype(F32) + update
        out[:, columns] = total.astype(BF16)


def shape(dims, dtype):
    return jax.ShapeDtypeStruct(dims, dtype)


def whole(dims):
    return pl.BlockSpec(dims, lambda step: (0,) * len(dims))


def body(
    grad_a_parts,
    grad_b_parts,
    factor_a,
    moment_a,
    factor_b,
    moment_b,
    base_down,
    slot_hidden,
    expert_ids,
    combine_weights,
):
    n_dp = lax.axis_size("dp")
    n_tensor = lax.axis_size("tensor")
    n_chips = n_tensor // 2
    same_core = [[chip * 2 + core for chip in range(n_chips)] for core in range(2)]
    pairs = [[chip * 2, chip * 2 + 1] for chip in range(n_chips)]
    swap = [(index, index ^ 1) for index in range(n_tensor)]
    cross = [
        ((a * n_chips + b) * 2 + core, (b * n_chips + a) * 2 + core)
        for a in range(n_dp)
        for b in range(n_chips)
        for core in range(2)
    ]
    packed = pl.pallas_call(
        pack_kernel,
        out_shape=shape((OWNERS, CHUNK, 128), BF16),
    )(grad_a_parts, grad_b_parts)
    parts = lax.all_to_all(packed, "dp", 0, 0, tiled=True)
    new_a, new_b, send_a, send_b = pl.pallas_call(
        step_kernel,
        out_shape=(
            shape((RANK, 128), F32),
            shape((B_ROWS, RANK), F32),
            shape((RANK, 128), BF16),
            shape((16, 128), BF16),
        ),
    )(parts, factor_a, moment_a, factor_b, moment_b)
    crossed = lax.ppermute(send_a, ("dp", "tensor"), cross)
    steps = WIDTH // TILE
    tile = pl.BlockSpec((HALF, TILE), lambda step: (0, step))
    send, own, rows, row_weights = pl.pallas_call(
        base_kernel,
        grid=(steps,),
        in_specs=[
            whole((TOKENS, 8)),
            whole((TOKENS, 8)),
            whole((SLOTS, 384)),
            pl.BlockSpec((384, TILE), lambda step: (0, step)),
        ],
        out_specs=[tile, tile, whole((TOKENS, 384)), whole((TOKENS, 128))],
        out_shape=(
            shape((HALF, WIDTH), BF16),
            shape((HALF, WIDTH), BF16),
            shape((TOKENS, 384), BF16),
            shape((TOKENS, 128), F32),
        ),
        scratch_shapes=[pltpu.VMEM((TOKENS, 128), F32) for _ in range(3)],
        cost_estimate=pl.CostEstimate(
            flops=2 * TOKENS * 384 * WIDTH, bytes_accessed=6 * 1024 * 1024, transcendentals=0
        ),
    )(expert_ids, combine_weights, slot_hidden, base_down)
    other = lax.ppermute(send, "tensor", swap)
    chunk = jnp.concatenate([crossed, send_b], axis=0)
    spread = jnp.broadcast_to(chunk[None], (n_dp, CHUNK, 128))
    gathered = lax.all_to_all(spread, "dp", 0, 0, tiled=True)
    packet, low = pl.pallas_call(
        low_rank_kernel,
        out_shape=(shape((OWNERS * RANK + 32, 128), BF16), shape((HALF, RANK), F32)),
        scratch_shapes=[pltpu.VMEM((OWNERS * B_ROWS, RANK), F32)],
    )(gathered, rows, row_weights)
    packets = lax.all_gather(packet, "tensor", axis_index_groups=pairs)
    joined = pl.pallas_call(
        join_kernel,
        grid=(steps,),
        in_specs=[whole((2, OWNERS * RANK + 32, 128)), whole((HALF, RANK)), tile, tile],
        out_specs=tile,
        out_shape=shape((HALF, WIDTH), BF16),
    )(packets, low, own, other)
    partials = lax.all_to_all(
        joined.reshape(CHIPS, 8, WIDTH), "tensor", 0, 0, tiled=True, axis_index_groups=same_core
    )
    scored = jnp.sum(partials.astype(F32), axis=0).astype(BF16)
    return new_a, new_b, scored


def solution(mesh):
    placed = (
        P("dp", None, "tensor"),
        P("dp", "tensor", None),
        P("dp", "tensor"),
        P("dp", "tensor"),
        P(("tensor", "dp"), None),
        P(("tensor", "dp"), None),
        P("tensor", None),
        P("dp", "tensor"),
        P("dp", None),
        P("dp", None),
    )
    return jax.shard_map(
        body,
        mesh=mesh,
        in_specs=placed,
        out_specs=(P("dp", "tensor"), P(("tensor", "dp"), None), P(("dp", "tensor"), None)),
        check_vma=False,
    )
```

```python
import jax
import jax.numpy as jnp
from jax import lax
from jax.experimental import pallas as pl
from jax.experimental.pallas import tpu as pltpu
from jax.sharding import PartitionSpec as P

MOMENTUM = 0.9
RATE = 0.5
RANK = 32
B_ROWS = 24
CHUNK = 48
OWNERS = 16
SLOTS = 192
TOKENS = 256
HIDDEN = 384
WIDTH = 4096
QUARTER = 1024
TILE = 1024
RING = 8
F32 = jnp.float32
BF16 = jnp.bfloat16


def pack_b(block):
    tail = jnp.concatenate([block[16:24], jnp.zeros((8, RANK), F32)], axis=0)
    return jnp.concatenate([block[0:16], tail, jnp.zeros((16, 64), F32)], axis=1)


def pack_kernel(grad_a, grad_b, out):
    columns = grad_b[0].T
    for owner in range(OWNERS):
        out[owner, 0:RANK, :] = grad_a[0, owner * RANK : (owner + 1) * RANK, :].astype(BF16)
        block = columns[owner * B_ROWS : (owner + 1) * B_ROWS, :]
        out[owner, RANK:CHUNK, :] = pack_b(block).astype(BF16)


def step_kernel(parts, factor_a, moment_a, factor_b, moment_b, new_a, new_b, spread):
    total = parts[0].astype(F32)
    for owner in range(1, OWNERS):
        total = total + parts[owner].astype(F32)
    stepped_a = factor_a[...] - RATE * (MOMENTUM * moment_a[...] + total[0:RANK])
    grad_b = jnp.concatenate([total[RANK:CHUNK, 0:32], total[RANK : RANK + 8, 32:64]], axis=0)
    stepped_b = factor_b[...] - RATE * (MOMENTUM * moment_b[...] + grad_b)
    new_a[...] = stepped_a
    new_b[...] = stepped_b
    chunk = jnp.concatenate([stepped_a, pack_b(stepped_b)], axis=0).astype(BF16)
    for owner in range(OWNERS):
        spread[owner] = chunk


def base_kernel(after, ids, weights, hidden, base, send, own, rows, row_weights):
    index = lax.axis_index("tensor")
    expert, core = index // 2, index % 2

    @pl.when(pl.program_id(0) == 0)
    def _():
        named = ids[...] == expert
        hit = jnp.sum(jnp.where(named, 1.0, 0.0), axis=0, keepdims=True)
        weight = jnp.sum(jnp.where(named, weights[...], 0.0), axis=0, keepdims=True)
        row = lax.broadcasted_iota(jnp.int32, (TOKENS, TOKENS), 0)
        column = lax.broadcasted_iota(jnp.int32, (TOKENS, TOKENS), 1)
        earlier = jnp.where(row < column, 1.0, 0.0).astype(BF16)
        wide = jnp.broadcast_to(hit, (8, TOKENS)).astype(BF16)
        before = jnp.dot(wide, earlier, preferred_element_type=F32)[0:1]
        slot = jnp.where(hit > 0.5, before, -1.0)
        both = jnp.concatenate([slot, weight, jnp.zeros((6, TOKENS), F32)], axis=0).T
        slots = lax.broadcasted_iota(jnp.int32, (TOKENS, SLOTS), 1)
        chosen = jnp.where(both[:, 0:1].astype(jnp.int32) == slots, 1.0, 0.0).astype(BF16)
        rows[...] = jnp.dot(chosen, hidden[...], preferred_element_type=F32).astype(BF16)
        row_weights[...] = jnp.broadcast_to(both[:, 1:2], (TOKENS, 128))

    part = jnp.dot(rows[...], base[...], preferred_element_type=F32) * row_weights[:, 0:1]
    for mine in range(2):

        @pl.when(core == mine)
        def _(mine=mine):
            for block in range(TILE // 128):
                ring, low, side = block // 4, block // 2 % 2, block % 2
                piece = part[:, block * 128 : (block + 1) * 128]
                columns = slice(ring * 128, (ring + 1) * 128)
                if side == mine:
                    own[low, :, columns] = piece
                else:
                    send[low, :, columns] = piece.astype(BF16)


def middle_kernel(own, other, send, keep):
    low = lax.axis_index("tensor") // 2 % 2
    send[...] = (own[1 - low] + other[1 - low].astype(F32)).astype(BF16)
    keep[...] = own[low] + other[low].astype(F32)


def low_rank_kernel(gathered, rows, row_weights, packet, b_scr):
    for owner in range(OWNERS):
        block = gathered[owner, RANK:CHUNK, :].astype(F32)
        b_scr[owner * B_ROWS : owner * B_ROWS + 16, :] = block[:, 0:32]
        b_scr[owner * B_ROWS + 16 : (owner + 1) * B_ROWS, :] = block[0:8, 32:64]
    low = jnp.dot(rows[...], b_scr[...].astype(BF16), preferred_element_type=F32)
    low = low * row_weights[:, 0:1]
    packet[...] = jnp.concatenate([low[at : at + 64] for at in range(0, TOKENS, 64)], axis=1).astype(BF16)


def join_kernel(packets, factors, keep, other, out):
    sides = []
    for low in range(2):
        total = packets[2 * low].astype(F32) + packets[2 * low + 1].astype(F32)
        sides.append(jnp.concatenate([total[:, at : at + 32] for at in range(0, 128, 32)], axis=0))
    low = jnp.concatenate(sides, axis=1).astype(BF16)
    for pair in range(RING // 2):
        halves = []
        for ring in (2 * pair, 2 * pair + 1):
            halves.append(
                jnp.concatenate([factors[ring, 0:RANK, :], factors[ring, CHUNK : CHUNK + RANK, :]], axis=0)
            )
        factor = jnp.concatenate(halves, axis=1)
        columns = slice(pair * 256, (pair + 1) * 256)
        update = jnp.dot(low, factor, preferred_element_type=F32)
        out[:, columns] = (keep[:, columns] + other[:, columns].astype(F32) + update).astype(BF16)


def add_kernel(parts, out):
    for part in range(4):
        total = parts[part].astype(F32)
        for ring in range(1, RING):
            total = total + parts[ring * 4 + part].astype(F32)
        for ring in range(RING):
            block = ring * 4 + part
            out[:, block * 128 : (block + 1) * 128] = total[:, ring * 128 : (ring + 1) * 128].astype(BF16)


def shape(dims, dtype):
    return jax.ShapeDtypeStruct(dims, dtype)


def whole(dims):
    return pl.BlockSpec(dims, lambda step: (0,) * len(dims))


def body(
    grad_a_parts,
    grad_b_parts,
    factor_a,
    moment_a,
    factor_b,
    moment_b,
    base_down,
    slot_hidden,
    expert_ids,
    combine_weights,
):
    n_tensor = lax.axis_size("tensor")
    quads = [[4 * ring + part for part in range(4)] for ring in range(n_tensor // 4)]
    rings = [[4 * ring + part for ring in range(n_tensor // 4)] for part in range(4)]
    packed = pl.pallas_call(
        pack_kernel,
        out_shape=shape((OWNERS, CHUNK, 128), BF16),
    )(grad_a_parts, jnp.swapaxes(grad_b_parts, 1, 2))
    parts = lax.all_to_all(packed, "dp", 0, 0, tiled=True)
    steps = WIDTH // TILE
    halves = pl.BlockSpec((2, TOKENS, TILE // 4), lambda step: (0, 0, step))
    send, own, rows, row_weights = pl.pallas_call(
        base_kernel,
        grid=(steps,),
        in_specs=[
            pl.BlockSpec(memory_space=pl.ANY),
            whole((8, TOKENS)),
            whole((8, TOKENS)),
            whole((SLOTS, HIDDEN)),
            pl.BlockSpec((HIDDEN, TILE), lambda step: (0, step)),
        ],
        out_specs=[halves, halves, whole((TOKENS, HIDDEN)), whole((TOKENS, 128))],
        out_shape=(
            shape((2, TOKENS, QUARTER), BF16),
            shape((2, TOKENS, QUARTER), F32),
            shape((TOKENS, HIDDEN), BF16),
            shape((TOKENS, 128), F32),
        ),
        cost_estimate=pl.CostEstimate(
            flops=2 * TOKENS * HIDDEN * WIDTH, bytes_accessed=7 * 1024 * 1024, transcendentals=0
        ),
    )(packed, expert_ids.T, combine_weights.T, slot_hidden, base_down)
    other = lax.ppermute(send, "tensor", [(index, index ^ 1) for index in range(n_tensor)])
    new_a, new_b, spread = pl.pallas_call(
        step_kernel,
        out_shape=(
            shape((RANK, 128), F32),
            shape((B_ROWS, RANK), F32),
            shape((OWNERS, CHUNK, 128), BF16),
        ),
    )(parts, factor_a, moment_a, factor_b, moment_b)
    gathered = lax.all_to_all(spread, "dp", 0, 0, tiled=True)
    send_low, keep = pl.pallas_call(
        middle_kernel,
        out_shape=(shape((TOKENS, QUARTER), BF16), shape((TOKENS, QUARTER), F32)),
        cost_estimate=pl.CostEstimate(flops=2**20, bytes_accessed=4 * 2**20, transcendentals=0),
    )(own, other)
    other_low = lax.ppermute(send_low, "tensor", [(index, index ^ 2) for index in range(n_tensor)])
    factors = lax.all_to_all(
        gathered.reshape(RING, 2 * CHUNK, 128), "tensor", 0, 0, tiled=True, axis_index_groups=rings
    )
    packet = pl.pallas_call(
        low_rank_kernel,
        out_shape=shape((64, 128), BF16),
        scratch_shapes=[pltpu.VMEM((OWNERS * B_ROWS, RANK), F32)],
    )(gathered, rows, row_weights)
    packets = lax.all_gather(packet, "tensor", axis_index_groups=quads)
    joined = pl.pallas_call(
        join_kernel,
        out_shape=shape((TOKENS, QUARTER), BF16),
    )(packets, factors, keep, other_low)
    partials = lax.all_to_all(joined.reshape(n_tensor, 8, QUARTER), "tensor", 0, 0, tiled=True)
    scored = pl.pallas_call(
        add_kernel,
        out_shape=shape((8, WIDTH), BF16),
    )(partials)
    return new_a, new_b, scored


def solution(mesh):
    placed = (
        P("dp", None, "tensor"),
        P("dp", "tensor", None),
        P("dp", "tensor"),
        P("dp", "tensor"),
        P(("tensor", "dp"), None),
        P(("tensor", "dp"), None),
        P("tensor", None),
        P("dp", "tensor"),
        P("dp", None),
        P("dp", None),
    )
    return jax.shard_map(
        body,
        mesh=mesh,
        in_specs=placed,
        out_specs=(P("dp", "tensor"), P(("tensor", "dp"), None), P(("dp", "tensor"), None)),
        check_vma=False,
    )
```

```python
import jax
import jax.numpy as jnp
from jax import lax
from jax.experimental import pallas as pl
from jax.experimental.pallas import tpu as pltpu
from jax.sharding import PartitionSpec as P

MOMENTUM = 0.9
RATE = 0.5
RANK = 32
B_ROWS = 24
CHUNK = 48
OWNERS = 16
SLOTS = 192
TOKENS = 256
HIDDEN = 384
WIDTH = 4096
QUARTER = 1024
TILE = 1024
RING = 8
F32 = jnp.float32
BF16 = jnp.bfloat16


def pack_b(block):
    tail = jnp.concatenate([block[16:24], jnp.zeros((8, RANK), F32)], axis=0)
    return jnp.concatenate([block[0:16], tail, jnp.zeros((16, 64), F32)], axis=1)


def first_rows(a, b):
    return lax.dot_general(a, b, (((0,), (0,)), ((), ())), preferred_element_type=F32)


def pack_kernel(grad_a, grad_b, out):
    columns = grad_b[0].T
    for owner in range(OWNERS):
        out[owner, 0:RANK, :] = grad_a[0, owner * RANK : (owner + 1) * RANK, :].astype(BF16)
        block = columns[owner * B_ROWS : (owner + 1) * B_ROWS, :]
        out[owner, RANK:CHUNK, :] = pack_b(block).astype(BF16)


def step_kernel(parts, factor_a, moment_a, factor_b, moment_b, new_a, new_b, spread):
    total = parts[0].astype(F32)
    for owner in range(1, OWNERS):
        total = total + parts[owner].astype(F32)
    stepped_a = factor_a[...] - RATE * (MOMENTUM * moment_a[...] + total[0:RANK])
    grad_b = jnp.concatenate([total[RANK:CHUNK, 0:32], total[RANK : RANK + 8, 32:64]], axis=0)
    stepped_b = factor_b[...] - RATE * (MOMENTUM * moment_b[...] + grad_b)
    new_a[...] = stepped_a
    new_b[...] = stepped_b
    chunk = jnp.concatenate([stepped_a, pack_b(stepped_b)], axis=0).astype(BF16)
    for owner in range(OWNERS):
        spread[owner] = chunk


def base_kernel(after, ids, weights, hidden, base, send, own, rows_t, row_weights, rows, column):
    index = lax.axis_index("tensor")
    expert, core = index // 2, index % 2

    @pl.when(pl.program_id(0) == 0)
    def _():
        named = ids[...] == expert
        hit = jnp.sum(jnp.where(named, 1.0, 0.0), axis=0, keepdims=True)
        weight = jnp.sum(jnp.where(named, weights[...], 0.0), axis=0, keepdims=True)
        one = lax.broadcasted_iota(jnp.int32, (TOKENS, TOKENS), 0)
        two = lax.broadcasted_iota(jnp.int32, (TOKENS, TOKENS), 1)
        earlier = jnp.where(one < two, 1.0, 0.0).astype(BF16)
        wide = jnp.broadcast_to(hit, (8, TOKENS)).astype(BF16)
        before = jnp.dot(wide, earlier, preferred_element_type=F32)[0:1]
        slot = jnp.where(hit > 0.5, before, -1.0)
        both = jnp.concatenate([slot, weight, jnp.zeros((6, TOKENS), F32)], axis=0).T
        slots = lax.broadcasted_iota(jnp.int32, (TOKENS, SLOTS), 1)
        chosen = jnp.where(both[:, 0:1].astype(jnp.int32) == slots, 1.0, 0.0).astype(BF16)
        rows[...] = jnp.dot(chosen, hidden[...], preferred_element_type=F32).astype(BF16)
        column[...] = jnp.broadcast_to(both[:, 1:2], (TOKENS, 128))
        slots_t = lax.broadcasted_iota(jnp.int32, (SLOTS, TOKENS), 0)
        chosen_t = jnp.where(slot.astype(jnp.int32) == slots_t, 1.0, 0.0).astype(BF16)
        rows_t[...] = first_rows(hidden[...], chosen_t).astype(BF16)
        row_weights[...] = jnp.broadcast_to(weight, (8, TOKENS))

    part = jnp.dot(rows[...], base[...], preferred_element_type=F32) * column[:, 0:1]
    for mine in range(2):

        @pl.when(core == mine)
        def _(mine=mine):
            for block in range(TILE // 128):
                ring, low, side = block // 4, block // 2 % 2, block % 2
                piece = part[:, block * 128 : (block + 1) * 128]
                columns = slice(ring * 128, (ring + 1) * 128)
                if side == mine:
                    own[low, :, columns] = piece
                else:
                    send[low, :, columns] = piece.astype(BF16)


def middle_kernel(own, other, send, keep):
    low = lax.axis_index("tensor") // 2 % 2
    send[...] = (own[1 - low] + other[1 - low].astype(F32)).astype(BF16)
    keep[...] = own[low] + other[low].astype(F32)


def low_rank_kernel(gathered, rows_t, row_weights, low, b_scr):
    for owner in range(OWNERS):
        block = gathered[owner, RANK:CHUNK, :].astype(F32)
        b_scr[owner * B_ROWS : owner * B_ROWS + 16, :] = block[:, 0:32]
        b_scr[owner * B_ROWS + 16 : (owner + 1) * B_ROWS, :] = block[0:8, 32:64]
    low[...] = (first_rows(b_scr[...].astype(BF16), rows_t[...]) * row_weights[0:1, :]).astype(BF16)


def join_kernel(lows, factors, keep, other, out):
    sides = [lows[2 * side].astype(F32) + lows[2 * side + 1].astype(F32) for side in range(2)]
    low = jnp.concatenate(sides, axis=0).astype(BF16)
    for pair in range(RING // 2):
        halves = [
            jnp.concatenate([factors[ring, 0:RANK, :], factors[ring, CHUNK : CHUNK + RANK, :]], axis=0)
            for ring in (2 * pair, 2 * pair + 1)
        ]
        columns = slice(pair * 256, (pair + 1) * 256)
        update = first_rows(low, jnp.concatenate(halves, axis=1))
        out[:, columns] = (keep[:, columns] + other[:, columns].astype(F32) + update).astype(BF16)


def add_kernel(parts, out):
    for part in range(4):
        total = parts[part].astype(F32)
        for ring in range(1, RING):
            total = total + parts[ring * 4 + part].astype(F32)
        for ring in range(RING):
            block = ring * 4 + part
            out[:, block * 128 : (block + 1) * 128] = total[:, ring * 128 : (ring + 1) * 128].astype(BF16)


def shape(dims, dtype):
    return jax.ShapeDtypeStruct(dims, dtype)


def whole(dims):
    return pl.BlockSpec(dims, lambda step: (0,) * len(dims))


def body(
    grad_a_parts,
    grad_b_parts,
    factor_a,
    moment_a,
    factor_b,
    moment_b,
    base_down,
    slot_hidden,
    expert_ids,
    combine_weights,
):
    n_tensor = lax.axis_size("tensor")
    quads = [[4 * ring + part for part in range(4)] for ring in range(n_tensor // 4)]
    rings = [[4 * ring + part for ring in range(n_tensor // 4)] for part in range(4)]
    packed = pl.pallas_call(
        pack_kernel,
        out_shape=shape((OWNERS, CHUNK, 128), BF16),
    )(grad_a_parts, jnp.swapaxes(grad_b_parts, 1, 2))
    parts = lax.all_to_all(packed, "dp", 0, 0, tiled=True)
    steps = WIDTH // TILE
    halves = pl.BlockSpec((2, TOKENS, TILE // 4), lambda step: (0, 0, step))
    send, own, rows_t, row_weights = pl.pallas_call(
        base_kernel,
        grid=(steps,),
        in_specs=[
            pl.BlockSpec(memory_space=pl.ANY),
            whole((8, TOKENS)),
            whole((8, TOKENS)),
            whole((SLOTS, HIDDEN)),
            pl.BlockSpec((HIDDEN, TILE), lambda step: (0, step)),
        ],
        out_specs=[halves, halves, whole((HIDDEN, TOKENS)), whole((8, TOKENS))],
        out_shape=(
            shape((2, TOKENS, QUARTER), BF16),
            shape((2, TOKENS, QUARTER), F32),
            shape((HIDDEN, TOKENS), BF16),
            shape((8, TOKENS), F32),
        ),
        scratch_shapes=[pltpu.VMEM((TOKENS, HIDDEN), BF16), pltpu.VMEM((TOKENS, 128), F32)],
        cost_estimate=pl.CostEstimate(
            flops=2 * TOKENS * HIDDEN * WIDTH, bytes_accessed=7 * 1024 * 1024, transcendentals=0
        ),
    )(packed, expert_ids.T, combine_weights.T, slot_hidden, base_down)
    new_a, new_b, spread = pl.pallas_call(
        step_kernel,
        out_shape=(
            shape((RANK, 128), F32),
            shape((B_ROWS, RANK), F32),
            shape((OWNERS, CHUNK, 128), BF16),
        ),
    )(parts, factor_a, moment_a, factor_b, moment_b)
    spread, send = lax.optimization_barrier((spread, send))
    other = lax.ppermute(send, "tensor", [(index, index ^ 1) for index in range(n_tensor)])
    gathered = lax.all_to_all(spread, "dp", 0, 0, tiled=True)
    send_low, keep = pl.pallas_call(
        middle_kernel,
        out_shape=(shape((TOKENS, QUARTER), BF16), shape((TOKENS, QUARTER), F32)),
        cost_estimate=pl.CostEstimate(flops=2**20, bytes_accessed=4 * 2**20, transcendentals=0),
    )(own, other)
    other_low = lax.ppermute(send_low, "tensor", [(index, index ^ 2) for index in range(n_tensor)])
    factors = lax.all_to_all(
        gathered.reshape(RING, 2 * CHUNK, 128), "tensor", 0, 0, tiled=True, axis_index_groups=rings
    )
    low = pl.pallas_call(
        low_rank_kernel,
        out_shape=shape((RANK, TOKENS), BF16),
        scratch_shapes=[pltpu.VMEM((OWNERS * B_ROWS, RANK), F32)],
    )(gathered, rows_t, row_weights)
    lows = lax.all_gather(low, "tensor", axis_index_groups=quads)
    joined = pl.pallas_call(
        join_kernel,
        out_shape=shape((TOKENS, QUARTER), BF16),
    )(lows, factors, keep, other_low)
    partials = lax.all_to_all(joined.reshape(n_tensor, 8, QUARTER), "tensor", 0, 0, tiled=True)
    scored = pl.pallas_call(
        add_kernel,
        out_shape=shape((8, WIDTH), BF16),
    )(partials)
    return new_a, new_b, scored


def solution(mesh):
    placed = (
        P("dp", None, "tensor"),
        P("dp", "tensor", None),
        P("dp", "tensor"),
        P("dp", "tensor"),
        P(("tensor", "dp"), None),
        P(("tensor", "dp"), None),
        P("tensor", None),
        P("dp", "tensor"),
        P("dp", None),
        P("dp", None),
    )
    return jax.shard_map(
        body,
        mesh=mesh,
        in_specs=placed,
        out_specs=(P("dp", "tensor"), P(("tensor", "dp"), None), P(("dp", "tensor"), None)),
        check_vma=False,
    )
```

```python
import jax
import jax.numpy as jnp
from jax import lax
from jax.experimental import pallas as pl
from jax.experimental.pallas import tpu as pltpu
from jax.sharding import PartitionSpec as P

MOMENTUM = 0.9
RATE = 0.5
RANK = 32
B_ROWS = 24
CHUNK = 48
OWNERS = 16
SLOTS = 192
TOKENS = 256
HIDDEN = 384
WIDTH = 4096
QUARTER = 1024
TILE = 1024
RING = 8
F32 = jnp.float32
BF16 = jnp.bfloat16


def pack_b(block):
    tail = jnp.concatenate([block[16:24], jnp.zeros((8, RANK), F32)], axis=0)
    return jnp.concatenate([block[0:16], tail, jnp.zeros((16, 64), F32)], axis=1)


def first_rows(a, b):
    return lax.dot_general(a, b, (((0,), (0,)), ((), ())), preferred_element_type=F32)


def pack_kernel(grad_a, grad_b, out):
    columns = grad_b[0].T
    for owner in range(OWNERS):
        out[owner, 0:RANK, :] = grad_a[0, owner * RANK : (owner + 1) * RANK, :].astype(BF16)
        block = columns[owner * B_ROWS : (owner + 1) * B_ROWS, :]
        out[owner, RANK:CHUNK, :] = pack_b(block).astype(BF16)


def step_kernel(parts, factor_a, moment_a, factor_b, moment_b, sum_a, sum_b, spread):
    total = parts[0].astype(F32)
    for owner in range(1, OWNERS):
        total = total + parts[owner].astype(F32)
    stepped_a = factor_a[...] - RATE * (MOMENTUM * moment_a[...] + total[0:RANK])
    grad_b = jnp.concatenate([total[RANK:CHUNK, 0:32], total[RANK : RANK + 8, 32:64]], axis=0)
    stepped_b = factor_b[...] - RATE * (MOMENTUM * moment_b[...] + grad_b)
    sum_a[...] = total[0:RANK]
    sum_b[...] = grad_b
    chunk = jnp.concatenate([stepped_a, pack_b(stepped_b)], axis=0).astype(BF16)
    for owner in range(OWNERS):
        spread[owner] = chunk


def output_kernel(sum_a, sum_b, factor_a, moment_a, factor_b, moment_b, new_a, new_b):
    new_a[...] = factor_a[...] - RATE * (MOMENTUM * moment_a[...] + sum_a[...])
    new_b[...] = factor_b[...] - RATE * (MOMENTUM * moment_b[...] + sum_b[...])


def base_kernel(after, ids, weights, hidden, base, send, own, rows_t, row_weights, rows, column):
    index = lax.axis_index("tensor")
    expert, core = index // 2, index % 2

    @pl.when(pl.program_id(0) == 0)
    def _():
        named = ids[...] == expert
        hit = jnp.sum(jnp.where(named, 1.0, 0.0), axis=0, keepdims=True)
        weight = jnp.sum(jnp.where(named, weights[...], 0.0), axis=0, keepdims=True)
        one = lax.broadcasted_iota(jnp.int32, (TOKENS, TOKENS), 0)
        two = lax.broadcasted_iota(jnp.int32, (TOKENS, TOKENS), 1)
        earlier = jnp.where(one < two, 1.0, 0.0).astype(BF16)
        wide = jnp.broadcast_to(hit, (8, TOKENS)).astype(BF16)
        before = jnp.dot(wide, earlier, preferred_element_type=F32)[0:1]
        slot = jnp.where(hit > 0.5, before, -1.0)
        both = jnp.concatenate([slot, weight, jnp.zeros((6, TOKENS), F32)], axis=0).T
        slots = lax.broadcasted_iota(jnp.int32, (TOKENS, SLOTS), 1)
        chosen = jnp.where(both[:, 0:1].astype(jnp.int32) == slots, 1.0, 0.0).astype(BF16)
        rows[...] = jnp.dot(chosen, hidden[...], preferred_element_type=F32).astype(BF16)
        column[...] = jnp.broadcast_to(both[:, 1:2], (TOKENS, 128))
        slots_t = lax.broadcasted_iota(jnp.int32, (SLOTS, TOKENS), 0)
        chosen_t = jnp.where(slot.astype(jnp.int32) == slots_t, 1.0, 0.0).astype(BF16)
        rows_t[...] = first_rows(hidden[...], chosen_t).astype(BF16)
        row_weights[...] = jnp.broadcast_to(weight, (8, TOKENS))

    part = jnp.dot(rows[...], base[...], preferred_element_type=F32) * column[:, 0:1]
    for mine in range(2):

        @pl.when(core == mine)
        def _(mine=mine):
            for block in range(TILE // 128):
                ring, low, side = block // 4, block // 2 % 2, block % 2
                piece = part[:, block * 128 : (block + 1) * 128]
                columns = slice(ring * 128, (ring + 1) * 128)
                if side == mine:
                    own[low, :, columns] = piece
                else:
                    send[low, :, columns] = piece.astype(BF16)


def middle_kernel(own, other, send, keep):
    low = lax.axis_index("tensor") // 2 % 2
    send[...] = (own[1 - low] + other[1 - low].astype(F32)).astype(BF16)
    keep[...] = own[low] + other[low].astype(F32)


def low_rank_kernel(gathered, rows_t, row_weights, low, b_scr):
    for owner in range(OWNERS):
        block = gathered[owner, RANK:CHUNK, :].astype(F32)
        b_scr[owner * B_ROWS : owner * B_ROWS + 16, :] = block[:, 0:32]
        b_scr[owner * B_ROWS + 16 : (owner + 1) * B_ROWS, :] = block[0:8, 32:64]
    low[...] = (first_rows(b_scr[...].astype(BF16), rows_t[...]) * row_weights[0:1, :]).astype(BF16)


def join_kernel(lows, factors, keep, other, out):
    sides = [lows[2 * side].astype(F32) + lows[2 * side + 1].astype(F32) for side in range(2)]
    low = jnp.concatenate(sides, axis=0).astype(BF16)
    for pair in range(RING // 2):
        halves = [
            jnp.concatenate([factors[ring, 0:RANK, :], factors[ring, CHUNK : CHUNK + RANK, :]], axis=0)
            for ring in (2 * pair, 2 * pair + 1)
        ]
        columns = slice(pair * 256, (pair + 1) * 256)
        update = first_rows(low, jnp.concatenate(halves, axis=1))
        out[:, columns] = (keep[:, columns] + other[:, columns].astype(F32) + update).astype(BF16)


def add_kernel(parts, out):
    for part in range(4):
        total = parts[part].astype(F32)
        for ring in range(1, RING):
            total = total + parts[ring * 4 + part].astype(F32)
        for ring in range(RING):
            block = ring * 4 + part
            out[:, block * 128 : (block + 1) * 128] = total[:, ring * 128 : (ring + 1) * 128].astype(BF16)


def shape(dims, dtype):
    return jax.ShapeDtypeStruct(dims, dtype)


def whole(dims):
    return pl.BlockSpec(dims, lambda step: (0,) * len(dims))


def body(
    grad_a_parts,
    grad_b_parts,
    factor_a,
    moment_a,
    factor_b,
    moment_b,
    base_down,
    slot_hidden,
    expert_ids,
    combine_weights,
):
    n_tensor = lax.axis_size("tensor")
    quads = [[4 * ring + part for part in range(4)] for ring in range(n_tensor // 4)]
    rings = [[4 * ring + part for ring in range(n_tensor // 4)] for part in range(4)]
    packed = pl.pallas_call(
        pack_kernel,
        compiler_params=pltpu.CompilerParams(vmem_limit_bytes=4 * 2**20),
        out_shape=shape((OWNERS, CHUNK, 128), BF16),
    )(grad_a_parts, jnp.swapaxes(grad_b_parts, 1, 2))
    parts = lax.all_to_all(packed, "dp", 0, 0, tiled=True)
    steps = WIDTH // TILE
    halves = pl.BlockSpec((2, TOKENS, TILE // 4), lambda step: (0, 0, step))
    send, own, rows_t, row_weights = pl.pallas_call(
        base_kernel,
        compiler_params=pltpu.CompilerParams(vmem_limit_bytes=16 * 2**20),
        grid=(steps,),
        in_specs=[
            pl.BlockSpec(memory_space=pl.ANY),
            whole((8, TOKENS)),
            whole((8, TOKENS)),
            whole((SLOTS, HIDDEN)),
            pl.BlockSpec((HIDDEN, TILE), lambda step: (0, step)),
        ],
        out_specs=[halves, halves, whole((HIDDEN, TOKENS)), whole((8, TOKENS))],
        out_shape=(
            shape((2, TOKENS, QUARTER), BF16),
            shape((2, TOKENS, QUARTER), F32),
            shape((HIDDEN, TOKENS), BF16),
            shape((8, TOKENS), F32),
        ),
        scratch_shapes=[pltpu.VMEM((TOKENS, HIDDEN), BF16), pltpu.VMEM((TOKENS, 128), F32)],
        cost_estimate=pl.CostEstimate(
            flops=2 * TOKENS * HIDDEN * WIDTH, bytes_accessed=7 * 1024 * 1024, transcendentals=0
        ),
    )(packed, expert_ids.T, combine_weights.T, slot_hidden, base_down)
    sum_a, sum_b, spread = pl.pallas_call(
        step_kernel,
        compiler_params=pltpu.CompilerParams(vmem_limit_bytes=4 * 2**20),
        out_shape=(
            shape((RANK, 128), F32),
            shape((B_ROWS, RANK), F32),
            shape((OWNERS, CHUNK, 128), BF16),
        ),
    )(parts, factor_a, moment_a, factor_b, moment_b)
    spread, send = lax.optimization_barrier((spread, send))
    other = lax.ppermute(send, "tensor", [(index, index ^ 1) for index in range(n_tensor)])
    gathered = lax.all_to_all(spread, "dp", 0, 0, tiled=True)
    new_a, new_b = pl.pallas_call(
        output_kernel,
        compiler_params=pltpu.CompilerParams(vmem_limit_bytes=2 * 2**20),
        out_shape=(shape((RANK, 128), F32), shape((B_ROWS, RANK), F32)),
        cost_estimate=pl.CostEstimate(flops=2**34, bytes_accessed=2**17, transcendentals=0),
    )(sum_a, sum_b, factor_a, moment_a, factor_b, moment_b)
    own, new_a, new_b = lax.optimization_barrier((own, new_a, new_b))
    send_low, keep = pl.pallas_call(
        middle_kernel,
        compiler_params=pltpu.CompilerParams(vmem_limit_bytes=12 * 2**20),
        out_shape=(shape((TOKENS, QUARTER), BF16), shape((TOKENS, QUARTER), F32)),
        cost_estimate=pl.CostEstimate(flops=2**20, bytes_accessed=4 * 2**20, transcendentals=0),
    )(own, other)
    other_low = lax.ppermute(send_low, "tensor", [(index, index ^ 2) for index in range(n_tensor)])
    factors = lax.all_to_all(
        gathered.reshape(RING, 2 * CHUNK, 128), "tensor", 0, 0, tiled=True, axis_index_groups=rings
    )
    low = pl.pallas_call(
        low_rank_kernel,
        compiler_params=pltpu.CompilerParams(vmem_limit_bytes=4 * 2**20),
        out_shape=shape((RANK, TOKENS), BF16),
        scratch_shapes=[pltpu.VMEM((OWNERS * B_ROWS, RANK), F32)],
    )(gathered, rows_t, row_weights)
    lows = lax.all_gather(low, "tensor", axis_index_groups=quads)
    joined = pl.pallas_call(
        join_kernel,
        compiler_params=pltpu.CompilerParams(vmem_limit_bytes=8 * 2**20),
        out_shape=shape((TOKENS, QUARTER), BF16),
    )(lows, factors, keep, other_low)
    partials = lax.all_to_all(joined.reshape(n_tensor, 8, QUARTER), "tensor", 0, 0, tiled=True)
    scored = pl.pallas_call(
        add_kernel,
        compiler_params=pltpu.CompilerParams(vmem_limit_bytes=4 * 2**20),
        out_shape=shape((8, WIDTH), BF16),
    )(partials)
    return new_a, new_b, scored


def solution(mesh):
    placed = (
        P("dp", None, "tensor"),
        P("dp", "tensor", None),
        P("dp", "tensor"),
        P("dp", "tensor"),
        P(("tensor", "dp"), None),
        P(("tensor", "dp"), None),
        P("tensor", None),
        P("dp", "tensor"),
        P("dp", None),
        P("dp", None),
    )
    return jax.shard_map(
        body,
        mesh=mesh,
        in_specs=placed,
        out_specs=(P("dp", "tensor"), P(("tensor", "dp"), None), P(("dp", "tensor"), None)),
        check_vma=False,
    )
```

```python
import jax
import jax.numpy as jnp
from jax import lax
from jax.experimental import pallas as pl
from jax.experimental.pallas import tpu as pltpu
from jax.sharding import PartitionSpec as P

MOMENTUM = 0.9
RATE = 0.5
RANK = 32
B_ROWS = 24
CHUNK = 48
OWNERS = 16
CHIPS = 16
SLOTS = 192
TOKENS = 256
HIDDEN = 384
WIDTH = 4096
SETS = 8
SET_WIDTH = 512
PAIR_WIDTH = 256
F32 = jnp.float32
BF16 = jnp.bfloat16


def pack_b(block):
    tail = jnp.concatenate([block[16:24], jnp.zeros((8, RANK), F32)], axis=0)
    return jnp.concatenate([block[0:16], tail, jnp.zeros((16, 64), F32)], axis=1)


def first_rows(a, b):
    return lax.dot_general(a, b, (((0,), (0,)), ((), ())), preferred_element_type=F32)


def pack_kernel(grad_a, grad_b, out):
    columns = grad_b[0].T
    for owner in range(OWNERS):
        out[owner, 0:RANK, :] = grad_a[0, owner * RANK : (owner + 1) * RANK, :].astype(BF16)
        block = columns[owner * B_ROWS : (owner + 1) * B_ROWS, :]
        out[owner, RANK:CHUNK, :] = pack_b(block).astype(BF16)


def step_kernel(parts, factor_a, moment_a, factor_b, moment_b, sum_a, sum_b, spread):
    total = parts[0].astype(F32)
    for owner in range(1, OWNERS):
        total = total + parts[owner].astype(F32)
    stepped_a = factor_a[...] - RATE * (MOMENTUM * moment_a[...] + total[0:RANK])
    grad_b = jnp.concatenate([total[RANK:CHUNK, 0:32], total[RANK : RANK + 8, 32:64]], axis=0)
    stepped_b = factor_b[...] - RATE * (MOMENTUM * moment_b[...] + grad_b)
    sum_a[...] = total[0:RANK]
    sum_b[...] = grad_b
    chunk = jnp.concatenate([stepped_a, pack_b(stepped_b)], axis=0).astype(BF16)
    for owner in range(OWNERS):
        spread[owner] = chunk


def output_kernel(sum_a, sum_b, factor_a, moment_a, factor_b, moment_b, new_a, new_b):
    new_a[...] = factor_a[...] - RATE * (MOMENTUM * moment_a[...] + sum_a[...])
    new_b[...] = factor_b[...] - RATE * (MOMENTUM * moment_b[...] + sum_b[...])


def base_kernel(after, ids, weights, hidden, base, send, own, rows_t, row_weights, rows, column):
    index = lax.axis_index("tensor")
    expert, core = index // 2, index % 2
    named = ids[...] == expert
    hit = jnp.sum(jnp.where(named, 1.0, 0.0), axis=0, keepdims=True)
    weight = jnp.sum(jnp.where(named, weights[...], 0.0), axis=0, keepdims=True)
    one = lax.broadcasted_iota(jnp.int32, (TOKENS, TOKENS), 0)
    two = lax.broadcasted_iota(jnp.int32, (TOKENS, TOKENS), 1)
    earlier = jnp.where(one < two, 1.0, 0.0).astype(BF16)
    wide = jnp.broadcast_to(hit, (8, TOKENS)).astype(BF16)
    before = jnp.dot(wide, earlier, preferred_element_type=F32)[0:1]
    slot = jnp.where(hit > 0.5, before, -1.0)
    both = jnp.concatenate([slot, weight, jnp.zeros((6, TOKENS), F32)], axis=0).T
    slots = lax.broadcasted_iota(jnp.int32, (TOKENS, SLOTS), 1)
    chosen = jnp.where(both[:, 0:1].astype(jnp.int32) == slots, 1.0, 0.0).astype(BF16)
    rows[...] = jnp.dot(chosen, hidden[...], preferred_element_type=F32).astype(BF16)
    column[...] = jnp.broadcast_to(both[:, 1:2], (TOKENS, 128))
    slots_t = lax.broadcasted_iota(jnp.int32, (SLOTS, TOKENS), 0)
    chosen_t = jnp.where(slot.astype(jnp.int32) == slots_t, 1.0, 0.0).astype(BF16)
    rows_t[...] = first_rows(hidden[...], chosen_t).astype(BF16)
    row_weights[...] = jnp.broadcast_to(weight, (8, TOKENS))
    for mine in range(2):

        @pl.when(core == mine)
        def _(mine=mine):
            for place in range(4):
                for side, out in ((1 - mine, send), (mine, own)):
                    at = (2 * place + side) * SET_WIDTH
                    part = jnp.dot(rows[...], base[:, at : at + SET_WIDTH], preferred_element_type=F32)
                    out[place] = (part * column[:, 0:1]).astype(BF16)


def middle_kernel(own, other, send_1, send_2, send_3, keep):
    place = lax.axis_index("tensor") // 2 % 4
    keep[...] = own[place].astype(F32) + other[place].astype(F32)
    low = place % 2
    flipped = (place + 1 - 2 * low, (place + 2) % 4, 3 - place)
    for there, send in zip(flipped, (send_1, send_2, send_3)):
        send[...] = (own[there].astype(F32) + other[there].astype(F32)).astype(BF16)


def low_rank_kernel(gathered, rows_t, row_weights, spread, b_scr):
    for owner in range(OWNERS):
        block = gathered[owner, RANK:CHUNK, :].astype(F32)
        b_scr[owner * B_ROWS : owner * B_ROWS + 16, :] = block[:, 0:32]
        b_scr[owner * B_ROWS + 16 : (owner + 1) * B_ROWS, :] = block[0:8, 32:64]
    low = (first_rows(b_scr[...].astype(BF16), rows_t[...]) * row_weights[0:1, :]).astype(BF16)
    for chip in range(CHIPS):
        spread[chip] = low


def sum_kernel(keep, other_1, other_2, other_3, out):
    total = keep[...]
    for other in (other_1, other_2, other_3):
        total = total + other[...].astype(F32)
    out[...] = total.astype(BF16)


def join_kernel(low, factors, base, out):
    blocks = [
        jnp.concatenate([factors[0, owner, 0:RANK, :], factors[1, owner, 0:RANK, :]], axis=1)
        for owner in range(OWNERS)
    ]
    update = first_rows(low[...], jnp.concatenate(blocks, axis=0))
    out[:, 0:SET_WIDTH] = base[...]
    out[:, SET_WIDTH:] = update.astype(BF16)


def add_kernel(parts, out):
    for group in range(SETS):
        total = parts[group, :, 0:SET_WIDTH].astype(F32)
        for ring in range(1, 4):
            total = total + parts[ring * SETS + group, :, 0:SET_WIDTH].astype(F32)
        for chip in (2 * group, 2 * group + 1):
            at = chip % 2 * PAIR_WIDTH
            update = parts[2 * chip, :, SET_WIDTH:].astype(F32) + parts[2 * chip + 1, :, SET_WIDTH:].astype(F32)
            columns = slice(chip * PAIR_WIDTH, (chip + 1) * PAIR_WIDTH)
            out[:, columns] = (total[:, at : at + PAIR_WIDTH] + update).astype(BF16)


def shape(dims, dtype):
    return jax.ShapeDtypeStruct(dims, dtype)


def body(
    grad_a_parts,
    grad_b_parts,
    factor_a,
    moment_a,
    factor_b,
    moment_b,
    base_down,
    slot_hidden,
    expert_ids,
    combine_weights,
):
    n_tensor = lax.axis_size("tensor")
    pairs = [[2 * chip, 2 * chip + 1] for chip in range(n_tensor // 2)]
    same_core = [[2 * chip + core for chip in range(n_tensor // 2)] for core in range(2)]

    def swap(array, bits):
        return lax.ppermute(array, "tensor", [(index, index ^ bits) for index in range(n_tensor)])

    vmem = pl.BlockSpec(memory_space=pltpu.VMEM)

    def limit(size):
        return pltpu.CompilerParams(vmem_limit_bytes=size * 2**20)

    def cost(flops, size):
        return pl.CostEstimate(flops=flops, bytes_accessed=size, transcendentals=0)

    packed = pl.pallas_call(
        pack_kernel,
        out_shape=shape((OWNERS, CHUNK, 128), BF16),
    )(grad_a_parts, jnp.swapaxes(grad_b_parts, 1, 2))
    parts = lax.all_to_all(packed, "dp", 0, 0, tiled=True)
    send, own, rows_t, row_weights = pl.pallas_call(
        base_kernel,
        in_specs=[pl.BlockSpec(memory_space=pl.ANY), vmem, vmem, vmem, vmem],
        out_shape=(
            shape((4, TOKENS, SET_WIDTH), BF16),
            shape((4, TOKENS, SET_WIDTH), BF16),
            shape((HIDDEN, TOKENS), BF16),
            shape((8, TOKENS), F32),
        ),
        scratch_shapes=[pltpu.VMEM((TOKENS, HIDDEN), BF16), pltpu.VMEM((TOKENS, 128), F32)],
        cost_estimate=cost(2 * TOKENS * HIDDEN * WIDTH, 7 * 2**20),
    )(packed, expert_ids.T, combine_weights.T, slot_hidden, base_down)
    other = swap(send, 1)
    sum_a, sum_b, spread = pl.pallas_call(
        step_kernel,
        out_shape=(
            shape((RANK, 128), F32),
            shape((B_ROWS, RANK), F32),
            shape((OWNERS, CHUNK, 128), BF16),
        ),
        compiler_params=limit(4),
        cost_estimate=cost(2**34, 2**18),
    )(parts, factor_a, moment_a, factor_b, moment_b)
    gathered = lax.all_to_all(spread, "dp", 0, 0, tiled=True)
    flat = shape((TOKENS, SET_WIDTH), BF16)
    send_1, send_2, send_3, keep = pl.pallas_call(
        middle_kernel,
        out_shape=(flat, flat, flat, shape((TOKENS, SET_WIDTH), F32)),
        compiler_params=limit(12),
        cost_estimate=cost(2**20, 4 * 2**20),
    )(own, other)
    others = [swap(send_1, 2), swap(send_2, 4), swap(send_3, 6)]
    low_spread = pl.pallas_call(
        low_rank_kernel,
        out_shape=shape((CHIPS, RANK, TOKENS), BF16),
        scratch_shapes=[pltpu.VMEM((OWNERS * B_ROWS, RANK), F32)],
        compiler_params=limit(4),
        cost_estimate=cost(2**34, 2**18),
    )(gathered, rows_t, row_weights)
    low_spread, sum_a = lax.optimization_barrier((low_spread, sum_a))
    new_a, new_b = pl.pallas_call(
        output_kernel,
        out_shape=(shape((RANK, 128), F32), shape((B_ROWS, RANK), F32)),
        compiler_params=limit(2),
    )(sum_a, sum_b, factor_a, moment_a, factor_b, moment_b)
    low = lax.all_to_all(low_spread, "tensor", 0, 0, tiled=True, axis_index_groups=same_core)
    factors = lax.all_gather(gathered, "tensor", axis_index_groups=pairs)
    keep, new_a, new_b = lax.optimization_barrier((keep, new_a, new_b))
    base = pl.pallas_call(
        sum_kernel,
        out_shape=flat,
        compiler_params=limit(8),
        cost_estimate=cost(2**34, 2**20),
    )(keep, *others)
    joined = pl.pallas_call(
        join_kernel,
        out_shape=shape((TOKENS, SET_WIDTH + PAIR_WIDTH), BF16),
        compiler_params=limit(8),
    )(low.reshape(CHIPS * RANK, TOKENS), factors, base)
    partials = lax.all_to_all(
        joined.reshape(n_tensor, 8, SET_WIDTH + PAIR_WIDTH), "tensor", 0, 0, tiled=True
    )
    scored = pl.pallas_call(
        add_kernel,
        out_shape=shape((8, WIDTH), BF16),
        compiler_params=limit(4),
    )(partials)
    return new_a, new_b, scored


def solution(mesh):
    placed = (
        P("dp", None, "tensor"),
        P("dp", "tensor", None),
        P("dp", "tensor"),
        P("dp", "tensor"),
        P(("tensor", "dp"), None),
        P(("tensor", "dp"), None),
        P("tensor", None),
        P("dp", "tensor"),
        P("dp", None),
        P("dp", None),
    )
    return jax.shard_map(
        body,
        mesh=mesh,
        in_specs=placed,
        out_specs=(P("dp", "tensor"), P(("tensor", "dp"), None), P(("dp", "tensor"), None)),
        check_vma=False,
    )
```

```python
import jax
import jax.numpy as jnp
from jax import lax
from jax.experimental import pallas as pl
from jax.experimental.pallas import tpu as pltpu
from jax.sharding import PartitionSpec as P

MOMENTUM = 0.9
RATE = 0.5
RANK = 32
B_ROWS = 24
CHUNK = 48
OWNERS = 16
CHIPS = 16
SLOTS = 192
TOKENS = 256
HIDDEN = 384
WIDTH = 4096
SETS = 8
SET_WIDTH = 512
PAIR_WIDTH = 256
F32 = jnp.float32
BF16 = jnp.bfloat16


def pack_b(block):
    tail = jnp.concatenate([block[16:24], jnp.zeros((8, RANK), F32)], axis=0)
    return jnp.concatenate([block[0:16], tail, jnp.zeros((16, 64), F32)], axis=1)


def first_rows(a, b):
    return lax.dot_general(a, b, (((0,), (0,)), ((), ())), preferred_element_type=F32)


def pack_kernel(grad_a, grad_b, out):
    columns = grad_b[0].T
    for owner in range(OWNERS):
        out[owner, 0:RANK, :] = grad_a[0, owner * RANK : (owner + 1) * RANK, :].astype(BF16)
        block = columns[owner * B_ROWS : (owner + 1) * B_ROWS, :]
        out[owner, RANK:CHUNK, :] = pack_b(block).astype(BF16)


def step_kernel(parts, factor_a, moment_a, factor_b, moment_b, sum_a, sum_b, spread):
    total = parts[0].astype(F32)
    for owner in range(1, OWNERS):
        total = total + parts[owner].astype(F32)
    stepped_a = factor_a[...] - RATE * (MOMENTUM * moment_a[...] + total[0:RANK])
    grad_b = jnp.concatenate([total[RANK:CHUNK, 0:32], total[RANK : RANK + 8, 32:64]], axis=0)
    stepped_b = factor_b[...] - RATE * (MOMENTUM * moment_b[...] + grad_b)
    sum_a[...] = total[0:RANK]
    sum_b[...] = grad_b
    chunk = jnp.concatenate([stepped_a, pack_b(stepped_b)], axis=0).astype(BF16)
    for owner in range(OWNERS):
        spread[owner] = chunk


def output_kernel(sum_a, sum_b, factor_a, moment_a, factor_b, moment_b, new_a, new_b):
    new_a[...] = factor_a[...] - RATE * (MOMENTUM * moment_a[...] + sum_a[...])
    new_b[...] = factor_b[...] - RATE * (MOMENTUM * moment_b[...] + sum_b[...])


def base_kernel(after, ids, weights, hidden, base, send, own, rows_t, row_weights, rows, column):
    index = lax.axis_index("tensor")
    expert, core = index // 2, index % 2

    @pl.when(pl.program_id(0) == 0)
    def _():
        named = ids[...] == expert
        hit = jnp.sum(jnp.where(named, 1.0, 0.0), axis=0, keepdims=True)
        weight = jnp.sum(jnp.where(named, weights[...], 0.0), axis=0, keepdims=True)
        one = lax.broadcasted_iota(jnp.int32, (TOKENS, TOKENS), 0)
        two = lax.broadcasted_iota(jnp.int32, (TOKENS, TOKENS), 1)
        earlier = jnp.where(one < two, 1.0, 0.0).astype(BF16)
        wide = jnp.broadcast_to(hit, (8, TOKENS)).astype(BF16)
        before = jnp.dot(wide, earlier, preferred_element_type=F32)[0:1]
        slot = jnp.where(hit > 0.5, before, -1.0)
        both = jnp.concatenate([slot, weight, jnp.zeros((6, TOKENS), F32)], axis=0).T
        slots = lax.broadcasted_iota(jnp.int32, (TOKENS, SLOTS), 1)
        chosen = jnp.where(both[:, 0:1].astype(jnp.int32) == slots, 1.0, 0.0).astype(BF16)
        rows[...] = jnp.dot(chosen, hidden[...], preferred_element_type=F32).astype(BF16)
        column[...] = jnp.broadcast_to(both[:, 1:2], (TOKENS, 128))
        slots_t = lax.broadcasted_iota(jnp.int32, (SLOTS, TOKENS), 0)
        chosen_t = jnp.where(slot.astype(jnp.int32) == slots_t, 1.0, 0.0).astype(BF16)
        rows_t[...] = first_rows(hidden[...], chosen_t).astype(BF16)
        row_weights[...] = jnp.broadcast_to(weight, (8, TOKENS))

    for mine in range(2):

        @pl.when(core == mine)
        def _(mine=mine):
            for place in range(2):
                for side, out in ((1 - mine, send), (mine, own)):
                    at = (2 * place + side) * SET_WIDTH
                    part = jnp.dot(rows[...], base[:, at : at + SET_WIDTH], preferred_element_type=F32)
                    out[place] = (part * column[:, 0:1]).astype(BF16)


def middle_kernel(own, other, send_1, send_2, send_3, keep):
    place = lax.axis_index("tensor") // 2 % 4
    keep[...] = own[place].astype(F32) + other[place].astype(F32)
    low = place % 2
    flipped = (place + 1 - 2 * low, (place + 2) % 4, 3 - place)
    for there, send in zip(flipped, (send_1, send_2, send_3)):
        send[...] = own[there] + other[there]


def low_rank_kernel(gathered, rows_t, row_weights, spread, b_scr):
    for owner in range(OWNERS):
        block = gathered[owner, RANK:CHUNK, :].astype(F32)
        b_scr[owner * B_ROWS : owner * B_ROWS + 16, :] = block[:, 0:32]
        b_scr[owner * B_ROWS + 16 : (owner + 1) * B_ROWS, :] = block[0:8, 32:64]
    low = (first_rows(b_scr[...].astype(BF16), rows_t[...]) * row_weights[0:1, :]).astype(BF16)
    for chip in range(CHIPS):
        spread[chip] = low


def sum_kernel(keep, other_1, other_2, other_3, out):
    total = keep[...]
    for other in (other_1, other_2, other_3):
        total = total + other[...].astype(F32)
    out[...] = total.astype(BF16)


def join_kernel(low, factors, base, out):
    blocks = [
        jnp.concatenate([factors[0, owner, 0:RANK, :], factors[1, owner, 0:RANK, :]], axis=1)
        for owner in range(OWNERS)
    ]
    update = first_rows(low[...], jnp.concatenate(blocks, axis=0))
    out[:, 0:SET_WIDTH] = base[...]
    out[:, SET_WIDTH:] = update.astype(BF16)


def add_kernel(parts, out):
    for group in range(SETS):
        total = parts[group, :, 0:SET_WIDTH].astype(F32)
        for ring in range(1, 4):
            total = total + parts[ring * SETS + group, :, 0:SET_WIDTH].astype(F32)
        for chip in (2 * group, 2 * group + 1):
            at = chip % 2 * PAIR_WIDTH
            update = parts[2 * chip, :, SET_WIDTH:].astype(F32) + parts[2 * chip + 1, :, SET_WIDTH:].astype(F32)
            columns = slice(chip * PAIR_WIDTH, (chip + 1) * PAIR_WIDTH)
            out[:, columns] = (total[:, at : at + PAIR_WIDTH] + update).astype(BF16)


def shape(dims, dtype):
    return jax.ShapeDtypeStruct(dims, dtype)


def body(
    grad_a_parts,
    grad_b_parts,
    factor_a,
    moment_a,
    factor_b,
    moment_b,
    base_down,
    slot_hidden,
    expert_ids,
    combine_weights,
):
    n_tensor = lax.axis_size("tensor")
    pairs = [[2 * chip, 2 * chip + 1] for chip in range(n_tensor // 2)]
    same_core = [[2 * chip + core for chip in range(n_tensor // 2)] for core in range(2)]

    def swap(array, bits):
        return lax.ppermute(array, "tensor", [(index, index ^ bits) for index in range(n_tensor)])

    half = pl.BlockSpec((2, TOKENS, SET_WIDTH), lambda step: (step, 0, 0))

    def whole(dims):
        return pl.BlockSpec(dims, lambda step: (0,) * len(dims))

    def limit(size):
        return pltpu.CompilerParams(vmem_limit_bytes=size * 2**20)

    def cost(flops, size):
        return pl.CostEstimate(flops=flops, bytes_accessed=size, transcendentals=0)

    packed = pl.pallas_call(
        pack_kernel,
        out_shape=shape((OWNERS, CHUNK, 128), BF16),
    )(grad_a_parts, jnp.swapaxes(grad_b_parts, 1, 2))
    parts = lax.all_to_all(packed, "dp", 0, 0, tiled=True)
    send, own, rows_t, row_weights = pl.pallas_call(
        base_kernel,
        grid=(2,),
        in_specs=[
            pl.BlockSpec(memory_space=pl.ANY),
            whole((8, TOKENS)),
            whole((8, TOKENS)),
            whole((SLOTS, HIDDEN)),
            pl.BlockSpec((HIDDEN, WIDTH // 2), lambda step: (0, step)),
        ],
        out_specs=[half, half, whole((HIDDEN, TOKENS)), whole((8, TOKENS))],
        out_shape=(
            shape((4, TOKENS, SET_WIDTH), BF16),
            shape((4, TOKENS, SET_WIDTH), BF16),
            shape((HIDDEN, TOKENS), BF16),
            shape((8, TOKENS), F32),
        ),
        scratch_shapes=[pltpu.VMEM((TOKENS, HIDDEN), BF16), pltpu.VMEM((TOKENS, 128), F32)],
        cost_estimate=cost(2 * TOKENS * HIDDEN * WIDTH, 7 * 2**20),
    )(packed, expert_ids.T, combine_weights.T, slot_hidden, base_down)
    other = swap(send, 1)
    sum_a, sum_b, spread = pl.pallas_call(
        step_kernel,
        out_shape=(
            shape((RANK, 128), F32),
            shape((B_ROWS, RANK), F32),
            shape((OWNERS, CHUNK, 128), BF16),
        ),
        compiler_params=limit(4),
        cost_estimate=cost(2**34, 2**18),
    )(parts, factor_a, moment_a, factor_b, moment_b)
    gathered = lax.all_to_all(spread, "dp", 0, 0, tiled=True)
    flat = shape((TOKENS, SET_WIDTH), BF16)
    send_1, send_2, send_3, keep = pl.pallas_call(
        middle_kernel,
        out_shape=(flat, flat, flat, shape((TOKENS, SET_WIDTH), F32)),
        compiler_params=limit(12),
        cost_estimate=cost(2**20, 4 * 2**20),
    )(own, other)
    others = [swap(send_1, 2), swap(send_2, 4), swap(send_3, 6)]
    low_spread = pl.pallas_call(
        low_rank_kernel,
        out_shape=shape((CHIPS, RANK, TOKENS), BF16),
        scratch_shapes=[pltpu.VMEM((OWNERS * B_ROWS, RANK), F32)],
        compiler_params=limit(4),
        cost_estimate=cost(2**34, 2**18),
    )(gathered, rows_t, row_weights)
    low_spread, sum_a = lax.optimization_barrier((low_spread, sum_a))
    new_a, new_b = pl.pallas_call(
        output_kernel,
        out_shape=(shape((RANK, 128), F32), shape((B_ROWS, RANK), F32)),
        compiler_params=limit(2),
    )(sum_a, sum_b, factor_a, moment_a, factor_b, moment_b)
    low = lax.all_to_all(low_spread, "tensor", 0, 0, tiled=True, axis_index_groups=same_core)
    factors = lax.all_gather(gathered, "tensor", axis_index_groups=pairs)
    keep, new_a, new_b = lax.optimization_barrier((keep, new_a, new_b))
    base = pl.pallas_call(
        sum_kernel,
        out_shape=flat,
        compiler_params=limit(8),
        cost_estimate=cost(2**34, 2**20),
    )(keep, *others)
    joined = pl.pallas_call(
        join_kernel,
        out_shape=shape((TOKENS, SET_WIDTH + PAIR_WIDTH), BF16),
        compiler_params=limit(8),
    )(low.reshape(CHIPS * RANK, TOKENS), factors, base)
    partials = lax.all_to_all(
        joined.reshape(n_tensor, 8, SET_WIDTH + PAIR_WIDTH), "tensor", 0, 0, tiled=True
    )
    scored = pl.pallas_call(
        add_kernel,
        out_shape=shape((8, WIDTH), BF16),
        compiler_params=limit(4),
    )(partials)
    return new_a, new_b, scored


def solution(mesh):
    placed = (
        P("dp", None, "tensor"),
        P("dp", "tensor", None),
        P("dp", "tensor"),
        P("dp", "tensor"),
        P(("tensor", "dp"), None),
        P(("tensor", "dp"), None),
        P("tensor", None),
        P("dp", "tensor"),
        P("dp", None),
        P("dp", None),
    )
    return jax.shard_map(
        body,
        mesh=mesh,
        in_specs=placed,
        out_specs=(P("dp", "tensor"), P(("tensor", "dp"), None), P(("dp", "tensor"), None)),
        check_vma=False,
    )
```

```python
import jax
import jax.numpy as jnp
from jax import lax
from jax.experimental import pallas as pl
from jax.experimental.pallas import tpu as pltpu
from jax.sharding import PartitionSpec as P

MOMENTUM = 0.9
RATE = 0.5
RANK = 32
B_ROWS = 24
CHUNK = 48
OWNERS = 16
CHIPS = 16
SLOTS = 192
TOKENS = 256
HIDDEN = 384
WIDTH = 4096
SETS = 8
SET_WIDTH = 512
PAIR_WIDTH = 256
F32 = jnp.float32
BF16 = jnp.bfloat16


def pack_b(block):
    tail = jnp.concatenate([block[16:24], jnp.zeros((8, RANK), F32)], axis=0)
    return jnp.concatenate([block[0:16], tail, jnp.zeros((16, 64), F32)], axis=1)


def first_rows(a, b):
    return lax.dot_general(a, b, (((0,), (0,)), ((), ())), preferred_element_type=F32)


def pack_kernel(grad_a, grad_b, out):
    columns = grad_b[0].T
    for owner in range(OWNERS):
        out[owner, 0:RANK, :] = grad_a[0, owner * RANK : (owner + 1) * RANK, :].astype(BF16)
        block = columns[owner * B_ROWS : (owner + 1) * B_ROWS, :]
        out[owner, RANK:CHUNK, :] = pack_b(block).astype(BF16)


def step_kernel(parts, factor_a, moment_a, factor_b, moment_b, sum_a, sum_b, spread):
    total = parts[0].astype(F32)
    for owner in range(1, OWNERS):
        total = total + parts[owner].astype(F32)
    stepped_a = factor_a[...] - RATE * (MOMENTUM * moment_a[...] + total[0:RANK])
    grad_b = jnp.concatenate([total[RANK:CHUNK, 0:32], total[RANK : RANK + 8, 32:64]], axis=0)
    stepped_b = factor_b[...] - RATE * (MOMENTUM * moment_b[...] + grad_b)
    sum_a[...] = total[0:RANK]
    sum_b[...] = grad_b
    chunk = jnp.concatenate([stepped_a, pack_b(stepped_b)], axis=0).astype(BF16)
    for owner in range(OWNERS):
        spread[owner] = chunk


def output_kernel(sum_a, sum_b, factor_a, moment_a, factor_b, moment_b, new_a, new_b):
    new_a[...] = factor_a[...] - RATE * (MOMENTUM * moment_a[...] + sum_a[...])
    new_b[...] = factor_b[...] - RATE * (MOMENTUM * moment_b[...] + sum_b[...])


def base_kernel(after, ids, weights, hidden, base, send, own, rows_t, row_weights, rows, column):
    index = lax.axis_index("tensor")
    expert, core = index // 2, index % 2

    @pl.when(pl.program_id(0) == 0)
    def _():
        named = ids[...] == expert
        hit = jnp.sum(jnp.where(named, 1.0, 0.0), axis=0, keepdims=True)
        weight = jnp.sum(jnp.where(named, weights[...], 0.0), axis=0, keepdims=True)
        one = lax.broadcasted_iota(jnp.int32, (TOKENS, TOKENS), 0)
        two = lax.broadcasted_iota(jnp.int32, (TOKENS, TOKENS), 1)
        earlier = jnp.where(one < two, 1.0, 0.0).astype(BF16)
        wide = jnp.broadcast_to(hit, (8, TOKENS)).astype(BF16)
        before = jnp.dot(wide, earlier, preferred_element_type=F32)[0:1]
        slot = jnp.where(hit > 0.5, before, -1.0)
        both = jnp.concatenate([slot, weight, jnp.zeros((6, TOKENS), F32)], axis=0).T
        slots = lax.broadcasted_iota(jnp.int32, (TOKENS, SLOTS), 1)
        chosen = jnp.where(both[:, 0:1].astype(jnp.int32) == slots, 1.0, 0.0).astype(BF16)
        rows[...] = jnp.dot(chosen, hidden[...], preferred_element_type=F32).astype(BF16)
        column[...] = jnp.broadcast_to(both[:, 1:2], (TOKENS, 128))
        slots_t = lax.broadcasted_iota(jnp.int32, (SLOTS, TOKENS), 0)
        chosen_t = jnp.where(slot.astype(jnp.int32) == slots_t, 1.0, 0.0).astype(BF16)
        rows_t[...] = first_rows(hidden[...], chosen_t).astype(BF16)
        row_weights[...] = jnp.broadcast_to(weight, (8, TOKENS))

    for mine in range(2):

        @pl.when(core == mine)
        def _(mine=mine):
            for place in range(2):
                for side, out in ((1 - mine, send), (mine, own)):
                    at = (2 * place + side) * SET_WIDTH
                    part = jnp.dot(rows[...], base[:, at : at + SET_WIDTH], preferred_element_type=F32)
                    out[place] = (part * column[:, 0:1]).astype(BF16)


def middle_kernel(own, other, send_1, send_2, send_3, keep):
    place = lax.axis_index("tensor") // 2 % 4
    keep[...] = own[place].astype(F32) + other[place].astype(F32)
    low = place % 2
    flipped = (place + 1 - 2 * low, (place + 2) % 4, 3 - place)
    for there, send in zip(flipped, (send_1, send_2, send_3)):
        send[...] = own[there] + other[there]


def low_rank_kernel(gathered, rows_t, row_weights, spread, b_scr):
    for owner in range(OWNERS):
        block = gathered[owner, RANK:CHUNK, :].astype(F32)
        b_scr[owner * B_ROWS : owner * B_ROWS + 16, :] = block[:, 0:32]
        b_scr[owner * B_ROWS + 16 : (owner + 1) * B_ROWS, :] = block[0:8, 32:64]
    low = (first_rows(b_scr[...].astype(BF16), rows_t[...]) * row_weights[0:1, :]).astype(BF16)
    for chip in range(CHIPS):
        spread[chip] = low


def sum_kernel(keep, other_1, other_2, other_3, out):
    total = keep[...]
    for other in (other_1, other_2, other_3):
        total = total + other[...].astype(F32)
    out[...] = total.astype(BF16)


def join_kernel(low, factors, base, out):
    blocks = [
        jnp.concatenate([factors[0, owner, 0:RANK, :], factors[1, owner, 0:RANK, :]], axis=1)
        for owner in range(OWNERS)
    ]
    update = first_rows(low[...], jnp.concatenate(blocks, axis=0))
    out[:, 0:SET_WIDTH] = base[...]
    out[:, SET_WIDTH:] = update.astype(BF16)


def add_kernel(parts, out):
    for group in range(SETS):
        total = parts[group, :, 0:SET_WIDTH].astype(F32)
        for ring in range(1, 4):
            total = total + parts[ring * SETS + group, :, 0:SET_WIDTH].astype(F32)
        for chip in (2 * group, 2 * group + 1):
            at = chip % 2 * PAIR_WIDTH
            update = parts[2 * chip, :, SET_WIDTH:].astype(F32) + parts[2 * chip + 1, :, SET_WIDTH:].astype(F32)
            columns = slice(chip * PAIR_WIDTH, (chip + 1) * PAIR_WIDTH)
            out[:, columns] = (total[:, at : at + PAIR_WIDTH] + update).astype(BF16)


def shape(dims, dtype):
    return jax.ShapeDtypeStruct(dims, dtype)


def body(
    grad_a_parts,
    grad_b_parts,
    factor_a,
    moment_a,
    factor_b,
    moment_b,
    base_down,
    slot_hidden,
    expert_ids,
    combine_weights,
):
    n_tensor = lax.axis_size("tensor")
    pairs = [[2 * chip, 2 * chip + 1] for chip in range(n_tensor // 2)]
    same_core = [[2 * chip + core for chip in range(n_tensor // 2)] for core in range(2)]

    def swap(array, bits):
        return lax.ppermute(array, "tensor", [(index, index ^ bits) for index in range(n_tensor)])

    half = pl.BlockSpec((2, TOKENS, SET_WIDTH), lambda step: (step, 0, 0))

    def whole(dims):
        return pl.BlockSpec(dims, lambda step: (0,) * len(dims))

    def limit(size):
        return pltpu.CompilerParams(vmem_limit_bytes=size * 2**20)

    def cost(flops, size):
        return pl.CostEstimate(flops=flops, bytes_accessed=size, transcendentals=0)

    packed = pl.pallas_call(
        pack_kernel,
        out_shape=shape((OWNERS, CHUNK, 128), BF16),
    )(grad_a_parts, jnp.swapaxes(grad_b_parts, 1, 2))
    parts = lax.all_to_all(packed, "dp", 0, 0, tiled=True)
    send, own, rows_t, row_weights = pl.pallas_call(
        base_kernel,
        grid=(2,),
        in_specs=[
            pl.BlockSpec(memory_space=pl.ANY),
            whole((8, TOKENS)),
            whole((8, TOKENS)),
            whole((SLOTS, HIDDEN)),
            pl.BlockSpec((HIDDEN, WIDTH // 2), lambda step: (0, step)),
        ],
        out_specs=[half, half, whole((HIDDEN, TOKENS)), whole((8, TOKENS))],
        out_shape=(
            shape((4, TOKENS, SET_WIDTH), BF16),
            shape((4, TOKENS, SET_WIDTH), BF16),
            shape((HIDDEN, TOKENS), BF16),
            shape((8, TOKENS), F32),
        ),
        scratch_shapes=[pltpu.VMEM((TOKENS, HIDDEN), BF16), pltpu.VMEM((TOKENS, 128), F32)],
        cost_estimate=cost(2 * TOKENS * HIDDEN * WIDTH, 7 * 2**20),
    )(packed, expert_ids.T, combine_weights.T, slot_hidden, base_down)
    other = swap(send, 1)
    sum_a, sum_b, spread = pl.pallas_call(
        step_kernel,
        out_shape=(
            shape((RANK, 128), F32),
            shape((B_ROWS, RANK), F32),
            shape((OWNERS, CHUNK, 128), BF16),
        ),
        compiler_params=limit(4),
        cost_estimate=cost(2**34, 2**18),
    )(parts, factor_a, moment_a, factor_b, moment_b)
    gathered = lax.all_to_all(spread, "dp", 0, 0, tiled=True)
    flat = shape((TOKENS, SET_WIDTH), BF16)
    send_1, send_2, send_3, keep = pl.pallas_call(
        middle_kernel,
        out_shape=(flat, flat, flat, shape((TOKENS, SET_WIDTH), F32)),
        compiler_params=limit(12),
        cost_estimate=cost(2**20, 4 * 2**20),
    )(own, other)
    others = [swap(send_3, 6), swap(send_2, 4), swap(send_1, 2)]
    low_spread = pl.pallas_call(
        low_rank_kernel,
        out_shape=shape((CHIPS, RANK, TOKENS), BF16),
        scratch_shapes=[pltpu.VMEM((OWNERS * B_ROWS, RANK), F32)],
        compiler_params=limit(4),
        cost_estimate=cost(2**34, 2**18),
    )(gathered, rows_t, row_weights)
    low_spread, sum_a = lax.optimization_barrier((low_spread, sum_a))
    new_a, new_b = pl.pallas_call(
        output_kernel,
        out_shape=(shape((RANK, 128), F32), shape((B_ROWS, RANK), F32)),
        compiler_params=limit(2),
    )(sum_a, sum_b, factor_a, moment_a, factor_b, moment_b)
    low = lax.all_to_all(low_spread, "tensor", 0, 0, tiled=True, axis_index_groups=same_core)
    factors = lax.all_gather(gathered, "tensor", axis_index_groups=pairs)
    keep, new_a, new_b = lax.optimization_barrier((keep, new_a, new_b))
    base = pl.pallas_call(
        sum_kernel,
        out_shape=flat,
        compiler_params=limit(8),
        cost_estimate=cost(2**34, 2**20),
    )(keep, *others)
    joined = pl.pallas_call(
        join_kernel,
        out_shape=shape((TOKENS, SET_WIDTH + PAIR_WIDTH), BF16),
        compiler_params=limit(8),
    )(low.reshape(CHIPS * RANK, TOKENS), factors, base)
    partials = lax.all_to_all(
        joined.reshape(n_tensor, 8, SET_WIDTH + PAIR_WIDTH), "tensor", 0, 0, tiled=True
    )
    scored = pl.pallas_call(
        add_kernel,
        out_shape=shape((8, WIDTH), BF16),
        compiler_params=limit(4),
    )(partials)
    return new_a, new_b, scored


def solution(mesh):
    placed = (
        P("dp", None, "tensor"),
        P("dp", "tensor", None),
        P("dp", "tensor"),
        P("dp", "tensor"),
        P(("tensor", "dp"), None),
        P(("tensor", "dp"), None),
        P("tensor", None),
        P("dp", "tensor"),
        P("dp", None),
        P("dp", None),
    )
    return jax.shard_map(
        body,
        mesh=mesh,
        in_specs=placed,
        out_specs=(P("dp", "tensor"), P(("tensor", "dp"), None), P(("dp", "tensor"), None)),
        check_vma=False,
    )
```
